32 devices in a mesh: batch: 32 (over z, y, x, core).
Axes of the slice: x: 2, y: 2, z: 4, core: 2. Of those that a mesh axis runs over, the one named last changes fastest.
Arguments:
- image_emb: bfloat16 [24576, 1152], P('batch'), may hold values from -300 to 300, as said below
- text_emb: bfloat16 [24576, 1152], P('batch'), may hold values from -300 to 300, as said below
- logit_scale: float32 [1], replicated, may hold values from 8 to 12
- logit_bias: float32 [1], replicated, may hold values from -3 to -1
Outputs:
- image_grad: bfloat16 [24576, 1152], P('batch')
- text_grad: bfloat16 [24576, 1152], P('batch')
The draws below stay inside these ranges and needn't reach their ends.
Inputs may be any that keep to these rules, and one draw needn't show every extreme that they name: `image_emb`: finite values, rows of differing magnitude. `text_emb`: finite values, rows of differing magnitude.
All inputs are finite; a program needn't handle non-finite values.
Results may differ from the reference program's by a relative error of at most 0.0034.
Values may be sent and summed in bfloat16 or wider, within the bound.
No kernel may reach another device: no remote copies, remote signals or barrier semaphores. Data moves between devices by JAX's collectives and lax.ppermute only.
A program may use at most 64 MiB of HBM per device.

```python
import math
import jax
import jax.numpy as jnp
from jax import lax

D = 1152
TOK_DEV = 768
STEPS = 4
TOKENS = 24576


latent_count = 8


def common_latent(key):
    key = jax.random.fold_in(key, 7)
    direction_key, weight_key = jax.random.split(key)
    directions = jnp.clip(jax.random.normal(direction_key, (latent_count, D), jnp.float32), -3.0, 3.0)
    weights = jnp.clip(jax.random.normal(weight_key, (TOKENS, latent_count), jnp.float32), -3.0, 3.0)
    return (directions, weights)


def mixed_latent(directions, weights):
    summed = jnp.zeros((TOKENS, D), jnp.float32)
    for which_dir in range(latent_count):
        summed = summed + weights[:, which_dir:which_dir + 1] * directions[which_dir:which_dir + 1, :]
    return summed * (1.0 / math.sqrt(latent_count))


def scaled_rows(key, latent):
    row_key, col_key, noise_key = jax.random.split(key, 3)
    columns = jnp.exp(jax.random.uniform(col_key, (1, D), jnp.float32, 0.0, 1.3863))
    row_scales = jnp.exp(jax.random.uniform(row_key, (TOKENS, 1), jnp.float32, 0.0, 2.3026))
    noise = jnp.clip(jax.random.normal(noise_key, (TOKENS, D), jnp.float32), -4.0, 4.0)
    values = (0.85 * latent + 0.55 * noise) * row_scales * columns
    return jnp.clip(values, -300.0, 300.0).astype(jnp.bfloat16)


def draw_image_emb(key, part):
    directions, weights = common_latent(key)
    key = jax.random.fold_in(key, 11)
    return scaled_rows(key, mixed_latent(directions, weights))


def draw_text_emb(key, part):
    directions, weights = common_latent(key)
    key = jax.random.fold_in(key, 23)
    own_key, kin_key, rest_key = jax.random.split(key, 3)
    own_weights = jnp.clip(jax.random.normal(own_key, (TOKENS, latent_count), jnp.float32), -3.0, 3.0)
    kinship = jax.random.uniform(kin_key, (TOKENS, 1), jnp.float32, 0.35, 0.85)
    text_weights = kinship * weights + jnp.sqrt(1.0 - kinship * kinship) * own_weights
    return scaled_rows(rest_key, mixed_latent(directions, text_weights))


def setup_inputs(seed: int = 0) -> dict:
    keys = jax.random.split(jax.random.key(seed), 5)
    image_emb = draw_image_emb(jax.random.fold_in(keys[4], 71), 0)
    text_emb = draw_text_emb(jax.random.fold_in(keys[4], 71), 0)
    logit_scale = jnp.clip(jax.random.uniform(keys[2], (1,), jnp.float32, 8.0, 12.0), 8.0, 12.0)
    logit_bias = jnp.clip(jax.random.uniform(keys[3], (1,), jnp.float32, -3.0, -1.0), -3.0, -1.0)
    return {"image_emb": image_emb, "text_emb": text_emb, "logit_scale": logit_scale, "logit_bias": logit_bias}


EPS = 1e-06

def unit_rows(raw):
    wide = raw.astype(jnp.float32)
    inv = lax.rsqrt(lax.optimization_barrier(jnp.sum(wide * wide, axis=-1, keepdims=True)) + EPS)
    return (wide * inv, inv)

def project_back(unit, inv, acc):
    along = lax.optimization_barrier(jnp.sum(unit * acc, axis=-1, keepdims=True))
    return (inv * (acc - unit * along)).astype(jnp.bfloat16)

def reference(image_emb, text_emb, logit_scale, logit_bias):
    blocks = TOKENS // TOK_DEV
    scale = logit_scale[0]
    bias = logit_bias[0]
    image_unit, image_inv = unit_rows(image_emb)
    text_unit, text_inv = unit_rows(text_emb)
    image_hat = image_unit.astype(jnp.bfloat16).reshape(blocks, TOK_DEV, D)
    text_hat = text_unit.astype(jnp.bfloat16).reshape(blocks, TOK_DEV, D)
    eye = jnp.eye(TOK_DEV, dtype=jnp.float32)
    image_acc = jnp.zeros((blocks, TOK_DEV, D), jnp.float32)
    text_acc = jnp.zeros((blocks, TOK_DEV, D), jnp.float32)
    for step in range(STEPS + 1):
        moved = jnp.roll(text_hat, step, axis=0)
        label = eye if step == 0 else jnp.zeros_like(eye)

        def one_block(pair):
            left, right = pair
            logits = scale * jnp.dot(left, right.T, preferred_element_type=jnp.float32) + bias
            coef = (jax.nn.sigmoid(logits) - label).astype(jnp.bfloat16)
            part_image = jnp.dot(coef, right, preferred_element_type=jnp.float32)
            part_text = jnp.dot(coef.T, left, preferred_element_type=jnp.float32)
            return (part_image, part_text)
        part_image, part_text = lax.map(one_block, (image_hat, moved))
        image_acc = image_acc + part_image
        text_acc = text_acc + jnp.roll(part_text, -step, axis=0)
    image_acc = (scale * image_acc).reshape(TOKENS, D)
    text_acc = (scale * text_acc).reshape(TOKENS, D)
    return (project_back(image_unit, image_inv, image_acc), project_back(text_unit, text_inv, text_acc))
```

```python
import functools

import jax
import jax.numpy as jnp
from jax import lax
from jax.experimental import pallas as pl
from jax.experimental.pallas import tpu as pltpu
from jax.sharding import PartitionSpec as P

EPS = 1e-06
CHUNKS = (384, 384)
ROW_TILE = 256
VMEM = pl.BlockSpec(memory_space=pltpu.VMEM)
SMEM = pl.BlockSpec(memory_space=pltpu.SMEM)
LIMIT = 32 * 1024 * 1024


def unit_rows(raw):
    wide = raw.astype(jnp.float32)
    inv = lax.rsqrt(jnp.sum(wide * wide, axis=-1, keepdims=True) + EPS)
    return wide * inv, inv


def hat_rows(raw):
    return unit_rows(raw)[0].astype(jnp.bfloat16)


def add_tile(total, own_hat, other_hat, scale, bias, first, diagonal=False):
    rows = own_hat.shape[0]
    other = other_hat[...]
    for start in range(0, rows, ROW_TILE):
        band = slice(start, start + ROW_TILE)
        logits = lax.dot_general(
            own_hat[band, :], other, (((1,), (1,)), ((), ())),
            preferred_element_type=jnp.float32,
        )
        coef = jax.nn.sigmoid(scale * logits + bias)
        if diagonal:
            i = lax.broadcasted_iota(jnp.int32, coef.shape, 0) + start
            j = lax.broadcasted_iota(jnp.int32, coef.shape, 1)
            coef = coef - jnp.where(i == j, 1.0, 0.0)
        part = jnp.dot(coef.astype(jnp.bfloat16), other, preferred_element_type=jnp.float32)
        if first:
            total[band, :] = part
        else:
            total[band, :] += part


def project_back(grad, total, raw, scale):
    rows = raw.shape[0]
    for start in range(0, rows, ROW_TILE):
        band = slice(start, start + ROW_TILE)
        unit, inv = unit_rows(raw[band, :])
        acc = scale * total[band, :]
        along = jnp.sum(unit * acc, axis=-1, keepdims=True)
        grad[band, :] = (inv * (acc - unit * along)).astype(jnp.bfloat16)


def own_kernel(scale_ref, bias_ref, u, v, u_hat, v_hat, u_total, v_total):
    scale, bias = scale_ref[0], bias_ref[0]
    u_hat[...] = hat_rows(u[...])
    v_hat[...] = hat_rows(v[...])
    add_tile(u_total, u_hat, v_hat, scale, bias, True, True)
    add_tile(v_total, v_hat, u_hat, scale, bias, True, True)


def step_kernel(far_first, scale_ref, bias_ref, flag, hat, total_in, near, near_twin, far, far_twin, twin, total, other):
    scale, bias = scale_ref[0], bias_ref[0]
    total[...] = total_in[...]
    blocks(far_first, scale, bias, flag, hat, near, near_twin, far, far_twin, twin, total, other)


def blocks(take_far, scale, bias, flag, hat, near, near_twin, far, far_twin, twin, total, other):
    for ref in (near, far, near_twin):
        other[...] = hat_rows(ref[...])
        add_tile(total, hat, other, scale, bias, False)

    @pl.when(flag[0] == take_far)
    def _():
        other[...] = hat_rows(far_twin[...])

    @pl.when(flag[0] != take_far)
    def _():
        other[...] = hat_rows(twin[...])

    add_tile(total, hat, other, scale, bias, False)


def mid_kernel(take_far, scale_ref, bias_ref, flag, hat, total_in, raw, near, near_twin, far, far_twin, twin, grad, total, other):
    scale, bias = scale_ref[0], bias_ref[0]
    total[...] = total_in[...]
    blocks(take_far, scale, bias, flag, hat, near, near_twin, far, far_twin, twin, total, other)
    project_back(grad, total, raw, scale)


def last_kernel(take_far, scale_ref, bias_ref, flag, hat, total_in, raw, near, near_twin, far, far_twin, twin, done, image_grad, text_grad, total, other):
    scale, bias = scale_ref[0], bias_ref[0]
    total[...] = total_in[...]
    blocks(take_far, scale, bias, flag, hat, near, near_twin, far, far_twin, twin, total, other)

    @pl.when(flag[1] == 0)
    def _():
        text_grad[...] = done[...]
        project_back(image_grad, total, raw, scale)

    @pl.when(flag[1] != 0)
    def _():
        image_grad[...] = done[...]
        project_back(text_grad, total, raw, scale)


def cost(products, rows, width, other):
    return pl.CostEstimate(flops=products * 2 * rows * width * other, bytes_accessed=0, transcendentals=0)


def shards(image, text, logit_scale, logit_bias):
    devices = lax.axis_size("batch")
    rows, width = image.shape
    me = lax.axis_index("batch")
    core, odd = lax.rem(me, 2), lax.rem(me // 2, 2)
    even = odd == 0
    flag = jnp.stack([jnp.where(core == odd, 0, 1), odd]).astype(jnp.int32)

    def send(block, pairs):
        return lax.ppermute(block, "batch", pairs)

    def is_odd(i):
        return (i // 2) % 2 == 1

    over_x = [(i, i ^ 2) for i in range(devices)]
    out_y = [(i, (i + (4 if is_odd(i) else -4)) % devices) for i in range(devices)]
    back_y = [(i, (i + (-4 if is_odd(i) else 4)) % devices) for i in range(devices)]
    in_chip = [(i, i ^ 1) for i in range(devices)]

    u = jnp.where(even, text, image)
    v = jnp.where(even, image, text)
    twin = send(jnp.where(core == 0, text, image), in_chip)
    bounds, at = [], 0
    for size in CHUNKS:
        bounds.append((at, at + size))
        at += size

    def call(body, outs, scratch, ins, products, other, alias=None):
        specs = [SMEM, SMEM] + [SMEM if a.ndim == 1 else VMEM for a in ins]
        return pl.pallas_call(
            body,
            out_shape=outs,
            in_specs=specs,
            out_specs=jax.tree.map(lambda _: VMEM, outs),
            scratch_shapes=scratch,
            compiler_params=pltpu.CompilerParams(vmem_limit_bytes=LIMIT),
            cost_estimate=cost(products, rows, width, other),
        )(logit_scale, logit_bias, *ins)

    hat_type = jax.ShapeDtypeStruct((rows, width), jnp.bfloat16)
    sum_type = jax.ShapeDtypeStruct((rows, width), jnp.float32)
    p1x = [send(u[a:b], over_x) for a, b in bounds]
    p1y = [send(v[a:b], out_y) for a, b in bounds]
    u_hat, v_hat, u_total, v_total = call(
        own_kernel, (hat_type, hat_type, sum_type, sum_type), [], (u, v), 4, rows
    )
    p2x, p2y = [], []
    for k, (a, b) in enumerate(bounds):
        mine, _ = lax.optimization_barrier((u[a:b], p1y[k]))
        relay, _ = lax.optimization_barrier((p1y[k], p1x[k]))
        p2x.append(send(relay, over_x))
        p2y.append(send(mine, back_y))
    s1x = [send(block, in_chip) for block in p1x]
    s1y = [send(block, in_chip) for block in p1y]
    s2x = [send(block, in_chip) for block in p2x]
    s2y = [send(block, in_chip) for block in p2y]

    def scratch(size):
        return pltpu.VMEM((size, width), jnp.bfloat16)

    last = len(bounds) - 1
    for k, (a, b) in enumerate(bounds):
        landed = (p1x[k], s1x[k], p1y[k], s1y[k], twin[a:b])
        if k < last:
            u_total = call(
                functools.partial(step_kernel, 1), sum_type, [scratch(b - a)],
                (flag, u_hat, u_total, *landed), 8, b - a,
            )
        else:
            u_grad = call(
                functools.partial(mid_kernel, 1), hat_type,
                [pltpu.VMEM((rows, width), jnp.float32), scratch(b - a)],
                (flag, u_hat, u_total, u, *landed), 8, b - a,
            )
    for k, (a, b) in enumerate(bounds):
        landed = (p2x[k], s2x[k], p2y[k], s2y[k], twin[a:b])
        if k < last:
            v_total = call(
                functools.partial(step_kernel, 0), sum_type, [scratch(b - a)],
                (flag, v_hat, v_total, *landed), 8, b - a,
            )
        else:
            return call(
                functools.partial(last_kernel, 0), (hat_type, hat_type),
                [pltpu.VMEM((rows, width), jnp.float32), scratch(b - a)],
                (flag, v_hat, v_total, v, *landed, u_grad), 8, b - a,
            )


def solution(mesh):
    placed = (P("batch", None), P("batch", None), P(), P())
    return jax.shard_map(
        shards,
        mesh=mesh,
        in_specs=placed,
        out_specs=(P("batch", None), P("batch", None)),
        check_vma=False,
    )
```

```python
import functools

import jax
import jax.numpy as jnp
from jax import lax
from jax.experimental import pallas as pl
from jax.experimental.pallas import tpu as pltpu
from jax.sharding import PartitionSpec as P

EPS = 1e-06
CHUNKS = (512, 256)
ROW_TILE = 256
VMEM = pl.BlockSpec(memory_space=pltpu.VMEM)
SMEM = pl.BlockSpec(memory_space=pltpu.SMEM)
MIB = 1024 * 1024
LIMITS = {"own": 20, "mid": 26, "step": 20, "last": 20}
BLOCK = 1024
COSTS = {"own": 4, "mid": 0, "step": 4, "last": 4}
ANY = pl.BlockSpec(memory_space=pl.ANY)


def unit_rows(raw):
    wide = raw.astype(jnp.float32)
    inv = lax.rsqrt(jnp.sum(wide * wide, axis=-1, keepdims=True) + EPS)
    return wide * inv, inv


def hat_rows(raw):
    return unit_rows(raw)[0].astype(jnp.bfloat16)


def bands(refs):
    at = 0
    for ref in refs:
        for start in range(0, ref.shape[0], ROW_TILE):
            yield slice(at, at + ROW_TILE), ref, slice(start, start + ROW_TILE)
            at += ROW_TILE


def add_tile(total, base, own_hat, other, scale, bias, diagonal=False, block=None):
    rows, count = own_hat.shape[0], other.shape[0]
    if block is not None:
        block = min(block, count)
        add_tile(total, base, own_hat, other.at[:block], scale, bias)

        @pl.loop(1, count // block)
        def _(k):
            part = other.at[pl.ds(pl.multiple_of(k * block, block), block)]
            add_tile(total, total, own_hat, part, scale, bias)

        return
    for start in range(0, rows, ROW_TILE):
        band = slice(start, start + ROW_TILE)
        logits = lax.dot_general(
            own_hat[band, :], other[...], (((1,), (1,)), ((), ())),
            preferred_element_type=jnp.float32,
        )
        coef = jax.nn.sigmoid(scale * logits + bias)
        if diagonal:
            i = lax.broadcasted_iota(jnp.int32, coef.shape, 0) + start
            j = lax.broadcasted_iota(jnp.int32, coef.shape, 1)
            coef = coef - jnp.where(i == j, 1.0, 0.0)
        part = jnp.dot(coef.astype(jnp.bfloat16), other[...], preferred_element_type=jnp.float32)
        total[band, :] = part if base is None else base[band, :] + part


def project_band(grad, total, band, raw, scale):
    unit, inv = unit_rows(raw)
    acc = scale * total[band, :]
    along = jnp.sum(unit * acc, axis=-1, keepdims=True)
    grad[band, :] = (inv * (acc - unit * along)).astype(jnp.bfloat16)


def project_back(grad, total, raw, scale):
    for band, ref, part in bands(raw):
        project_band(grad, total, band, ref[part, :], scale)


def put_hat(hat, raw, at=0):
    rows = raw.shape[0]
    for start in range(0, rows, ROW_TILE):
        stop = min(start + ROW_TILE, rows)
        hat[at + start:at + stop, :] = hat_rows(raw[start:stop, :])


def own_kernel(scale_ref, bias_ref, *refs):
    n = len(CHUNKS)
    u, v, (u_hat, v_hat, u_total, v_total) = refs[0], refs[1:1 + n], refs[1 + n:]
    scale, bias = scale_ref[0], bias_ref[0]
    put_hat(u_hat, u)
    at = 0
    for part in v:
        put_hat(v_hat, part, at)
        at += part.shape[0]
    add_tile(u_total, None, u_hat, v_hat, scale, bias, True)
    add_tile(v_total, None, v_hat, u_hat, scale, bias, True)


def gather_hats(other, flag, take_far, at, plain, far_twins, twin):
    row = 0
    for block in plain:
        put_hat(other, block, row)
        row += block.shape[0]
    for far_twin in far_twins:
        size = far_twin.shape[0]
        for start in range(0, size, ROW_TILE):
            stop = min(start + ROW_TILE, size)
            extra = jnp.where(
                flag[0] == take_far, far_twin[start:stop, :], twin[at + start:at + stop, :]
            )
            other[row + start:row + stop, :] = hat_rows(extra)
        row, at = row + size, at + size


def step_kernel(take_far, at, count, far, scale_ref, bias_ref, flag, hat, base, *refs):
    plain, far_twins, (twin, total, other) = refs[:count], refs[count:count + far], refs[count + far:]
    gather_hats(other, flag, take_far, at, plain, far_twins, twin)
    add_tile(total, base, hat, other, scale_ref[0], bias_ref[0], block=BLOCK)


def mid_kernel(take_far, at, count, far, scale_ref, bias_ref, flag, hat, base, *refs):
    plain, far_twins, refs = refs[:count], refs[count:count + far], refs[count + far:]
    twin, raw, grad, total, other = refs
    gather_hats(other, flag, take_far, at, plain, far_twins, twin)
    add_tile(total, base, hat, other, scale_ref[0], bias_ref[0], block=BLOCK)
    project_back(grad, total, (raw,), scale_ref[0])


def last_kernel(take_far, at, count, far, scale_ref, bias_ref, flag, hat, base, *refs):
    n = len(CHUNKS)
    plain, far_twins, refs = refs[:count], refs[count:count + far], refs[count + far:]
    twin, raw, (done, image_grad, text_grad, total, other, grad, sems) = refs[0], refs[1:1 + n], refs[1 + n:]
    is_image = flag[1] == 0
    scale = scale_ref[0]
    whole = (
        pltpu.make_async_copy(done, text_grad, sems.at[0]),
        pltpu.make_async_copy(done, image_grad, sems.at[0]),
    )

    def each(pair, act):
        @pl.when(is_image)
        def _():
            act(pair[0])

        @pl.when(jnp.logical_not(is_image))
        def _():
            act(pair[1])

    each(whole, lambda copy: copy.start())
    gather_hats(other, flag, take_far, at, plain, far_twins, twin)
    add_tile(total, base, hat, other, scale, bias_ref[0], block=BLOCK)
    copies, row = [], 0
    for k, ref in enumerate(raw):
        band = slice(row, row + ref.shape[0])
        row += ref.shape[0]
        project_band(grad, total, band, ref[...], scale)
        copies.append((
            pltpu.make_async_copy(grad.at[band], image_grad.at[band], sems.at[1 + k]),
            pltpu.make_async_copy(grad.at[band], text_grad.at[band], sems.at[1 + k]),
        ))
        each(copies[-1], lambda copy: copy.start())
    for pair in (whole, *copies):
        each(pair, lambda copy: copy.wait())


def after(value, *before):
    return lax.optimization_barrier((value, *before))[0]


def shards(image, text, logit_scale, logit_bias):
    devices = lax.axis_size("batch")
    rows, width = image.shape
    me = lax.axis_index("batch")
    core, odd = lax.rem(me, 2), lax.rem(me // 2, 2)
    flag = jnp.stack([jnp.where(core == odd, 0, 1), odd]).astype(jnp.int32)

    def send(block, pairs):
        return lax.ppermute(block, "batch", pairs)

    def is_odd(i):
        return (i // 2) % 2 == 1

    over_x = [(i, i ^ 2) for i in range(devices)]
    out_y = [(i, (i + (4 if is_odd(i) else -4)) % devices) for i in range(devices)]
    back_y = [(i, (i + (-4 if is_odd(i) else 4)) % devices) for i in range(devices)]
    in_chip = [(i, i ^ 1) for i in range(devices)]

    even = odd == 0
    n = len(CHUNKS)
    spans = [slice(sum(CHUNKS[:k]), sum(CHUNKS[:k + 1])) for k in range(n)]
    u = jnp.where(even, text, image)
    v = [jnp.where(even, image[span], text[span]) for span in spans]

    def call(kind, body, outs, scratch, ins, products, out_spec=VMEM):
        specs = [SMEM, SMEM] + [SMEM if a.ndim == 1 else VMEM for a in ins]
        return pl.pallas_call(
            body,
            out_shape=outs,
            in_specs=specs,
            out_specs=jax.tree.map(lambda _: out_spec, outs),
            scratch_shapes=scratch,
            compiler_params=pltpu.CompilerParams(vmem_limit_bytes=LIMITS[kind] * MIB),
            cost_estimate=pl.CostEstimate(
                flops=COSTS[kind] * rows * width * products, bytes_accessed=0, transcendentals=0
            ),
        )(logit_scale, logit_bias, *ins)

    hat_type = jax.ShapeDtypeStruct((rows, width), jnp.bfloat16)
    sum_type = jax.ShapeDtypeStruct((rows, width), jnp.float32)
    running = pltpu.VMEM((rows, width), jnp.float32)

    def room(size):
        return pltpu.VMEM((size, width), jnp.bfloat16)

    def named(name, block, pairs):
        with jax.named_scope(name):
            return send(block, pairs)

    def step(kind, take_far, start, hat, base, plain, far_twins, extra=()):
        size = sum(block.shape[0] for block in (*plain, *far_twins))
        ins = (flag, hat, base, *plain, *far_twins, twin, *extra)
        body, out, scratch, spec = {
            "step": (step_kernel, sum_type, [room(size)], VMEM),
            "mid": (mid_kernel, hat_type, [running, room(size)], VMEM),
            "last": (
                last_kernel, (hat_type, hat_type),
                [running, room(size), room(rows), pltpu.SemaphoreType.DMA((1 + n,))], ANY,
            ),
        }[kind]
        body = functools.partial(body, take_far, start, len(plain), len(far_twins))
        return call(kind, body, out, scratch, ins, size, spec)

    p1x = named("p1x", u, over_x)
    p1y = [named(f"p1y{k}", v[k], out_y) for k in range(n)]
    u_own, *u_part = lax.optimization_barrier((u, *(u[span] for span in spans)))
    u_hat, v_hat, u_total, v_total = call(
        "own", own_kernel, (hat_type, hat_type, sum_type, sum_type), [], (u_own, *v), rows * 2
    )
    late_text, late_image, _ = lax.optimization_barrier((text, image, u))
    twin = named("twin", jnp.where(core == 0, late_text, late_image), in_chip)
    p1x, twin, v_hat, *p1y = lax.optimization_barrier((p1x, twin, v_hat, *p1y))
    p2x, p2y = [None] * n, [None] * n
    for k in range(n):
        p2x[k] = named(f"p2x{k}", p1y[k], over_x)
        p2y[k] = named(f"p2y{k}", after(u_part[k], p1y[k]), back_y)
    s1x = named("s1x", p1x, in_chip)
    s1y = [named(f"s1y{k}", p1y[k], in_chip) for k in range(n)]
    u_grad = token = step("mid", 1, 0, u_hat, u_total, [p1x, s1x, *p1y], s1y, (u_own,))
    for k in range(n):
        near_twin = named(f"s2x{k}", after(p2x[k], token), in_chip)
        far_twin = named(f"s2y{k}", after(p2y[k], token), in_chip)
        plain, start = [p2x[k], p2y[k], near_twin], spans[k].start
        if k < n - 1:
            v_total = token = step("step", 0, start, v_hat, v_total, plain, [far_twin])
        else:
            return step("last", 0, start, v_hat, v_total, plain, [far_twin], (*v, u_grad))


def solution(mesh):
    placed = (P("batch", None), P("batch", None), P(), P())
    return jax.shard_map(
        shards,
        mesh=mesh,
        in_specs=placed,
        out_specs=(P("batch", None), P("batch", None)),
        check_vma=False,
    )
```

```python
import functools

import jax
import jax.numpy as jnp
from jax import lax
from jax.experimental import pallas as pl
from jax.experimental.pallas import tpu as pltpu
from jax.sharding import PartitionSpec as P

EPS = 1e-06
CHUNKS = (512, 256)
ROW_TILE = 256
TWIN = 384
OVER_X = (400, 368)
VMEM = pl.BlockSpec(memory_space=pltpu.VMEM)
SMEM = pl.BlockSpec(memory_space=pltpu.SMEM)
MIB = 1024 * 1024
LIMITS = {"half": 15, "own": 16, "mid": 20, "step": 20, "last": 20}
BLOCK = 1024
COSTS = {"half": 0, "own": 4, "mid": 0, "step": 4, "last": 4}
ANY = pl.BlockSpec(memory_space=pl.ANY)


def unit_rows(raw):
    wide = raw.astype(jnp.float32)
    inv = lax.rsqrt(jnp.sum(wide * wide, axis=-1, keepdims=True) + EPS)
    return wide * inv, inv


def hat_rows(raw):
    return unit_rows(raw)[0].astype(jnp.bfloat16)


def bands(refs):
    at = 0
    for ref in refs:
        count = ref.shape[0]
        for start in range(0, count, ROW_TILE):
            stop = min(start + ROW_TILE, count)
            yield slice(at + start, at + stop), ref, slice(start, stop)
        at += count


def add_tile(total, base, own_hat, other, scale, bias, diagonal=False, block=None):
    rows, count = own_hat.shape[0], other.shape[0]
    if block is not None:
        block = count // 2 if count > 1152 else count
        add_tile(total, base, own_hat, other.at[:block], scale, bias)

        @pl.loop(1, count // block)
        def _(k):
            part = other.at[pl.ds(pl.multiple_of(k * block, block), block)]
            add_tile(total, total, own_hat, part, scale, bias)

        return
    for start in range(0, rows, ROW_TILE):
        band = slice(start, start + ROW_TILE)
        logits = lax.dot_general(
            own_hat[band, :], other[...], (((1,), (1,)), ((), ())),
            preferred_element_type=jnp.float32,
        )
        coef = jax.nn.sigmoid(scale * logits + bias)
        if diagonal:
            i = lax.broadcasted_iota(jnp.int32, coef.shape, 0) + start
            j = lax.broadcasted_iota(jnp.int32, coef.shape, 1)
            coef = coef - jnp.where(i == j, 1.0, 0.0)
        part = jnp.dot(coef.astype(jnp.bfloat16), other[...], preferred_element_type=jnp.float32)
        total[band, :] = part if base is None else base[band, :] + part


def project_band(grad, total, band, raw, scale):
    unit, inv = unit_rows(raw)
    acc = scale * total[band, :]
    along = jnp.sum(unit * acc, axis=-1, keepdims=True)
    grad[band, :] = (inv * (acc - unit * along)).astype(jnp.bfloat16)


def project_back(grad, total, raw, scale):
    for band, ref, part in bands(raw):
        project_band(grad, total, band, ref[part, :], scale)


def put_hat(hat, raw, at=0):
    rows = raw.shape[0]
    for start in range(0, rows, ROW_TILE):
        stop = min(start + ROW_TILE, rows)
        hat[at + start:at + stop, :] = hat_rows(raw[start:stop, :])


def own_kernel(scale_ref, bias_ref, *refs):
    n, m = len(CHUNKS), len(OVER_X)
    u, v, (u_hat, v_hat, u_total, v_total) = refs[:m], refs[m:m + n], refs[m + n:]
    scale, bias = scale_ref[0], bias_ref[0]
    for hat, parts in ((u_hat, u), (v_hat, v)):
        at = 0
        for part in parts:
            put_hat(hat, part, at)
            at += part.shape[0]
    add_tile(u_total, None, u_hat, v_hat, scale, bias, True)
    add_tile(v_total, None, v_hat, u_hat, scale, bias, True)


def gather_hats(other, flag, take_far, plain, far_twins=(), twin=None, at=0, landing=()):
    row = 0
    for block in plain:
        put_hat(other, block, row)
        row += block.shape[0]
    first = row
    for copy in landing:
        copy.wait()
    for far_twin in far_twins:
        size = far_twin.shape[0]
        start = 0
        while start < size:
            own = row - first + start
            stop = min(size, start + min(ROW_TILE, TWIN - (at + own) % TWIN))
            extra = jnp.where(
                flag[0] == take_far, far_twin[start:stop, :], twin(own, stop - start)
            )
            other[row + start:row + stop, :] = hat_rows(extra)
            start = stop
        row += size


def rows_at(twin, at):
    def read(row, count):
        piece, here = divmod(at + row, TWIN)
        return twin[piece][here:here + count, :]

    return read


def fetch(twin, at, size, spare, sems):
    copies, row = [], 0
    while row < size:
        piece, here = divmod(at + row, TWIN)
        count = min(size - row, TWIN - here)
        copies.append(
            pltpu.make_async_copy(
                twin[piece].at[pl.ds(here, count)], spare.at[pl.ds(row, count)], sems.at[len(copies)]
            )
        )
        row += count
    for copy in copies:
        copy.start()
    return copies


def half_kernel(scale_ref, bias_ref, flag, hat, base, *refs):
    *plain, total, other = refs
    gather_hats(other, flag, 0, plain)
    add_tile(total, base, hat, other, scale_ref[0], bias_ref[0], block=BLOCK)


def step_kernel(take_far, at, count, far, scale_ref, bias_ref, flag, hat, base, *refs):
    plain, far_twins, (*twin, total, other) = refs[:count], refs[count:count + far], refs[count + far:]
    gather_hats(other, flag, take_far, plain, far_twins, rows_at(twin, at), at)
    add_tile(total, base, hat, other, scale_ref[0], bias_ref[0], block=BLOCK)


def mid_kernel(take_far, at, count, far, scale_ref, bias_ref, flag, hat, base, *refs):
    plain, far_twins, refs = refs[:count], refs[count:count + far], refs[count + far:]
    *refs, grad, total, other, spare, pieces = refs
    m = len(OVER_X)
    twin, raw = refs[:-m], refs[-m:]
    landing = fetch(twin, at, spare.shape[0], spare, pieces)
    gather_hats(
        other, flag, take_far, plain, far_twins,
        lambda row, size: spare[row:row + size, :], at, landing,
    )
    add_tile(total, base, hat, other, scale_ref[0], bias_ref[0], block=BLOCK)
    project_back(grad, total, raw, scale_ref[0])


def last_kernel(take_far, at, count, far, scale_ref, bias_ref, flag, hat, base, *refs):
    n = len(CHUNKS)
    plain, far_twins, refs = refs[:count], refs[count:count + far], refs[count + far:]
    *refs, done, image_grad, text_grad, total, other, grad, sems = refs
    twin, raw = refs[:-n], refs[-n:]
    is_image = flag[1] == 0
    scale = scale_ref[0]
    whole = (
        pltpu.make_async_copy(done, text_grad, sems.at[0]),
        pltpu.make_async_copy(done, image_grad, sems.at[0]),
    )

    def each(pair, act):
        @pl.when(is_image)
        def _():
            act(pair[0])

        @pl.when(jnp.logical_not(is_image))
        def _():
            act(pair[1])

    each(whole, lambda copy: copy.start())
    gather_hats(other, flag, take_far, plain, far_twins, rows_at(twin, at), at)
    add_tile(total, base, hat, other, scale, bias_ref[0], block=BLOCK)
    copies, row = [], 0
    for k, ref in enumerate(raw):
        band = slice(row, row + ref.shape[0])
        row += ref.shape[0]
        project_band(grad, total, band, ref[...], scale)
        copies.append((
            pltpu.make_async_copy(grad.at[band], image_grad.at[band], sems.at[1 + k]),
            pltpu.make_async_copy(grad.at[band], text_grad.at[band], sems.at[1 + k]),
        ))
        each(copies[-1], lambda copy: copy.start())
    for pair in (whole, *copies):
        each(pair, lambda copy: copy.wait())


def after(value, *before):
    return lax.optimization_barrier((value, *before))[0]


def shards(image, text, logit_scale, logit_bias):
    devices = lax.axis_size("batch")
    rows, width = image.shape
    me = lax.axis_index("batch")
    core, odd = lax.rem(me, 2), lax.rem(me // 2, 2)
    flag = jnp.stack([jnp.where(core == odd, 0, 1), odd]).astype(jnp.int32)

    def send(block, pairs):
        return lax.ppermute(block, "batch", pairs)

    def is_odd(i):
        return (i // 2) % 2 == 1

    over_x = [(i, i ^ 2) for i in range(devices)]
    out_y = [(i, (i + (4 if is_odd(i) else -4)) % devices) for i in range(devices)]
    back_y = [(i, (i + (-4 if is_odd(i) else 4)) % devices) for i in range(devices)]
    in_chip = [(i, i ^ 1) for i in range(devices)]

    even = odd == 0
    n = len(CHUNKS)
    spans = [slice(sum(CHUNKS[:k]), sum(CHUNKS[:k + 1])) for k in range(n)]
    cuts = [slice(sum(OVER_X[:k]), sum(OVER_X[:k + 1])) for k in range(len(OVER_X))]
    u = [jnp.where(even, text[cut], image[cut]) for cut in cuts]
    v = [jnp.where(even, image[span], text[span]) for span in spans]

    def call(kind, body, outs, scratch, ins, products, out_spec=VMEM, far=()):
        specs = [SMEM, SMEM] + [SMEM if a.ndim == 1 else VMEM for a in ins]
        for k in far:
            specs[2 + k] = ANY
        return pl.pallas_call(
            body,
            out_shape=outs,
            in_specs=specs,
            out_specs=jax.tree.map(lambda _: out_spec, outs),
            scratch_shapes=scratch,
            compiler_params=pltpu.CompilerParams(vmem_limit_bytes=LIMITS[kind] * MIB),
            cost_estimate=pl.CostEstimate(
                flops=COSTS[kind] * rows * width * products, bytes_accessed=0, transcendentals=0
            ),
        )(logit_scale, logit_bias, *ins)

    hat_type = jax.ShapeDtypeStruct((rows, width), jnp.bfloat16)
    sum_type = jax.ShapeDtypeStruct((rows, width), jnp.float32)
    running = pltpu.VMEM((rows, width), jnp.float32)

    def room(size):
        return pltpu.VMEM((size, width), jnp.bfloat16)

    def named(name, block, pairs):
        with jax.named_scope(name):
            return send(block, pairs)

    def step(kind, take_far, start, hat, base, plain, far_twins, extra=()):
        late = sum(block.shape[0] for block in far_twins)
        size = sum(block.shape[0] for block in plain) + late
        first = 3 + len(plain) + len(far_twins)
        ins = (flag, hat, base, *plain, *far_twins, *(twin if late else ()), *extra)
        body, out, scratch, spec = {
            "half": (half_kernel, sum_type, [room(size)], VMEM),
            "step": (step_kernel, sum_type, [room(size)], VMEM),
            "mid": (mid_kernel, hat_type, [running, room(size)], VMEM),
            "last": (
                last_kernel, (hat_type, hat_type),
                [running, room(size), room(rows), pltpu.SemaphoreType.DMA((1 + n,))], ANY,
            ),
        }[kind]
        if not late:
            return call(kind, body, out, scratch, ins, size, spec)
        body = functools.partial(body, take_far, start, len(plain), len(far_twins))
        if kind != "mid":
            return call(kind, body, out, scratch, ins, size, spec)
        scratch = [*scratch, room(late), pltpu.SemaphoreType.DMA((len(twin),))]
        return call(kind, body, out, scratch, ins, size, spec, range(first, first + len(twin)))

    p1y = [named(f"p1y{k}", v[k], out_y) for k in range(n)]
    p1x = [named(f"p1x{k}", part, over_x) for k, part in enumerate(u)]
    late_text, late_image, *_ = lax.optimization_barrier((text, image, v[0], *u))
    twin = []
    for start in range(0, rows, TWIN):
        here = slice(start, start + TWIN)
        mine = jnp.where(core == 0, late_text[here], late_image[here])
        twin.append(named(f"twin{start}", mine, in_chip))
    u_part = [jnp.where(even, late_text[span], late_image[span]) for span in spans]
    v_own, u_part = lax.optimization_barrier((v, u_part))
    u_hat, v_hat, u_total, v_total = call(
        "own", own_kernel, (hat_type, hat_type, sum_type, sum_type), [], (*u, *v_own), rows * 2
    )
    p1x, v_hat, p1y, twin, u_part = lax.optimization_barrier((p1x, v_hat, p1y, twin, u_part))
    p2x, p2y = [None] * n, [None] * n
    for k in range(n):
        p2x[k] = named(f"p2x{k}", p1y[k], over_x)
        p2y[k] = named(f"p2y{k}", after(u_part[k], p1y[k]), back_y)
    s1x = [named(f"s1x{k}", part, in_chip) for k, part in enumerate(p1x)]
    s1y = [named(f"s1y{k}", p1y[k], in_chip) for k in range(n)]
    u_total = step("half", 1, 0, u_hat, u_total, [*p1x, *p1y], [])
    u_grad = token = step("mid", 1, 0, u_hat, u_total, s1x, s1y, tuple(u))
    for k in range(n):
        near_twin = named(f"s2x{k}", after(p2x[k], token), in_chip)
        far_twin = named(f"s2y{k}", after(p2y[k], token), in_chip)
        plain, start = [p2x[k], p2y[k], near_twin], spans[k].start
        if k < n - 1:
            v_total = token = step("step", 0, start, v_hat, v_total, plain, [far_twin])
        else:
            return step("last", 0, start, v_hat, v_total, plain, [far_twin], (*v, u_grad))


def solution(mesh):
    placed = (P("batch", None), P("batch", None), P(), P())
    return jax.shard_map(
        shards,
        mesh=mesh,
        in_specs=placed,
        out_specs=(P("batch", None), P("batch", None)),
        check_vma=False,
    )
```

```python
import functools

import jax
import jax.numpy as jnp
from jax import lax
from jax.experimental import pallas as pl
from jax.experimental.pallas import tpu as pltpu
from jax.sharding import PartitionSpec as P

EPS = 1e-06
CHUNKS = (512, 256)
ROW_TILE = 256
TWIN = 384
OVER_X = (768,)
VMEM = pl.BlockSpec(memory_space=pltpu.VMEM)
SMEM = pl.BlockSpec(memory_space=pltpu.SMEM)
MIB = 1024 * 1024
LIMITS = {"half": 15, "own": 16, "mid": 20, "step": 20, "last": 20}
BLOCK = 1024
COSTS = {"half": 0, "own": 4, "mid": 0, "step": 4, "last": 4}
ANY = pl.BlockSpec(memory_space=pl.ANY)


def unit_rows(raw):
    wide = raw.astype(jnp.float32)
    inv = lax.rsqrt(jnp.sum(wide * wide, axis=-1, keepdims=True) + EPS)
    return wide * inv, inv


def hat_rows(raw):
    return unit_rows(raw)[0].astype(jnp.bfloat16)


def bands(refs):
    at = 0
    for ref in refs:
        count = ref.shape[0]
        for start in range(0, count, ROW_TILE):
            stop = min(start + ROW_TILE, count)
            yield slice(at + start, at + stop), ref, slice(start, stop)
        at += count


def add_tile(total, base, own_hat, other, scale, bias, diagonal=False, block=None):
    rows, count = own_hat.shape[0], other.shape[0]
    if block is not None:
        block = count // 2 if count > 1152 else count
        add_tile(total, base, own_hat, other.at[:block], scale, bias)

        @pl.loop(1, count // block)
        def _(k):
            part = other.at[pl.ds(pl.multiple_of(k * block, block), block)]
            add_tile(total, total, own_hat, part, scale, bias)

        return
    for start in range(0, rows, ROW_TILE):
        band = slice(start, start + ROW_TILE)
        logits = lax.dot_general(
            own_hat[band, :], other[...], (((1,), (1,)), ((), ())),
            preferred_element_type=jnp.float32,
        )
        coef = jax.nn.sigmoid(scale * logits + bias)
        if diagonal:
            i = lax.broadcasted_iota(jnp.int32, coef.shape, 0) + start
            j = lax.broadcasted_iota(jnp.int32, coef.shape, 1)
            coef = coef - jnp.where(i == j, 1.0, 0.0)
        part = jnp.dot(coef.astype(jnp.bfloat16), other[...], preferred_element_type=jnp.float32)
        total[band, :] = part if base is None else base[band, :] + part


def project_band(grad, total, band, raw, scale):
    unit, inv = unit_rows(raw)
    acc = scale * total[band, :]
    along = jnp.sum(unit * acc, axis=-1, keepdims=True)
    grad[band, :] = (inv * (acc - unit * along)).astype(jnp.bfloat16)


def project_back(grad, total, raw, scale):
    for band, ref, part in bands(raw):
        project_band(grad, total, band, ref[part, :], scale)


def put_hat(hat, raw, at=0):
    rows = raw.shape[0]
    for start in range(0, rows, ROW_TILE):
        stop = min(start + ROW_TILE, rows)
        hat[at + start:at + stop, :] = hat_rows(raw[start:stop, :])


def own_kernel(scale_ref, bias_ref, *refs):
    n, m = len(CHUNKS), len(OVER_X)
    u, v, (u_hat, v_hat, u_total, v_total) = refs[:m], refs[m:m + n], refs[m + n:]
    scale, bias = scale_ref[0], bias_ref[0]
    for hat, parts in ((u_hat, u), (v_hat, v)):
        at = 0
        for part in parts:
            put_hat(hat, part, at)
            at += part.shape[0]
    add_tile(u_total, None, u_hat, v_hat, scale, bias, True)
    add_tile(v_total, None, v_hat, u_hat, scale, bias, True)


def gather_hats(other, flag, take_far, plain, far_twins=(), twin=None, at=0, landing=()):
    row = 0
    for block in plain:
        put_hat(other, block, row)
        row += block.shape[0]
    first = row
    for copy in landing:
        copy.wait()
    for far_twin in far_twins:
        size = far_twin.shape[0]
        start = 0
        while start < size:
            own = row - first + start
            stop = min(size, start + min(ROW_TILE, TWIN - (at + own) % TWIN))
            extra = jnp.where(
                flag[0] == take_far, far_twin[start:stop, :], twin(own, stop - start)
            )
            other[row + start:row + stop, :] = hat_rows(extra)
            start = stop
        row += size


def rows_at(twin, at):
    def read(row, count):
        piece, here = divmod(at + row, TWIN)
        return twin[piece][here:here + count, :]

    return read


def fetch(twin, at, size, spare, sems):
    copies, row = [], 0
    while row < size:
        piece, here = divmod(at + row, TWIN)
        count = min(size - row, TWIN - here)
        copies.append(
            pltpu.make_async_copy(
                twin[piece].at[pl.ds(here, count)], spare.at[pl.ds(row, count)], sems.at[len(copies)]
            )
        )
        row += count
    for copy in copies:
        copy.start()
    return copies


def half_kernel(scale_ref, bias_ref, flag, hat, base, *refs):
    *plain, total, other = refs
    gather_hats(other, flag, 0, plain)
    add_tile(total, base, hat, other, scale_ref[0], bias_ref[0], block=BLOCK)


def step_kernel(take_far, at, count, far, scale_ref, bias_ref, flag, hat, base, *refs):
    plain, far_twins, (*twin, total, other) = refs[:count], refs[count:count + far], refs[count + far:]
    gather_hats(other, flag, take_far, plain, far_twins, rows_at(twin, at), at)
    add_tile(total, base, hat, other, scale_ref[0], bias_ref[0], block=BLOCK)


def mid_kernel(take_far, at, count, far, scale_ref, bias_ref, flag, hat, base, *refs):
    plain, far_twins, refs = refs[:count], refs[count:count + far], refs[count + far:]
    *refs, grad, total, other, spare, pieces = refs
    m = len(OVER_X)
    twin, raw = refs[:-m], refs[-m:]
    landing = fetch(twin, at, spare.shape[0], spare, pieces)
    gather_hats(
        other, flag, take_far, plain, far_twins,
        lambda row, size: spare[row:row + size, :], at, landing,
    )
    add_tile(total, base, hat, other, scale_ref[0], bias_ref[0], block=BLOCK)
    project_back(grad, total, raw, scale_ref[0])


def last_kernel(take_far, at, count, far, scale_ref, bias_ref, flag, hat, base, *refs):
    n = len(CHUNKS)
    plain, far_twins, refs = refs[:count], refs[count:count + far], refs[count + far:]
    *refs, done, image_grad, text_grad, total, other, grad, sems = refs
    twin, raw = refs[:-n], refs[-n:]
    is_image = flag[1] == 0
    scale = scale_ref[0]
    whole = (
        pltpu.make_async_copy(done, text_grad, sems.at[0]),
        pltpu.make_async_copy(done, image_grad, sems.at[0]),
    )

    def each(pair, act):
        @pl.when(is_image)
        def _():
            act(pair[0])

        @pl.when(jnp.logical_not(is_image))
        def _():
            act(pair[1])

    each(whole, lambda copy: copy.start())
    gather_hats(other, flag, take_far, plain, far_twins, rows_at(twin, at), at)
    add_tile(total, base, hat, other, scale, bias_ref[0], block=BLOCK)
    copies, row = [], 0
    for k, ref in enumerate(raw):
        band = slice(row, row + ref.shape[0])
        row += ref.shape[0]
        project_band(grad, total, band, ref[...], scale)
        copies.append((
            pltpu.make_async_copy(grad.at[band], image_grad.at[band], sems.at[1 + k]),
            pltpu.make_async_copy(grad.at[band], text_grad.at[band], sems.at[1 + k]),
        ))
        each(copies[-1], lambda copy: copy.start())
    for pair in (whole, *copies):
        each(pair, lambda copy: copy.wait())


def after(value, *before):
    return lax.optimization_barrier((value, *before))[0]


def shards(image, text, logit_scale, logit_bias):
    devices = lax.axis_size("batch")
    rows, width = image.shape
    me = lax.axis_index("batch")
    core, odd = lax.rem(me, 2), lax.rem(me // 2, 2)
    flag = jnp.stack([jnp.where(core == odd, 0, 1), odd]).astype(jnp.int32)

    def send(block, pairs):
        return lax.ppermute(block, "batch", pairs)

    def is_odd(i):
        return (i // 2) % 2 == 1

    over_x = [(i, i ^ 2) for i in range(devices)]
    out_y = [(i, (i + (4 if is_odd(i) else -4)) % devices) for i in range(devices)]
    back_y = [(i, (i + (-4 if is_odd(i) else 4)) % devices) for i in range(devices)]
    in_chip = [(i, i ^ 1) for i in range(devices)]

    even = odd == 0
    n = len(CHUNKS)
    spans = [slice(sum(CHUNKS[:k]), sum(CHUNKS[:k + 1])) for k in range(n)]
    cuts = [slice(sum(OVER_X[:k]), sum(OVER_X[:k + 1])) for k in range(len(OVER_X))]
    u = [jnp.where(even, text[cut], image[cut]) for cut in cuts]
    v = [jnp.where(even, image[span], text[span]) for span in spans]

    def call(kind, body, outs, scratch, ins, products, out_spec=VMEM, far=()):
        specs = [SMEM, SMEM] + [SMEM if a.ndim == 1 else VMEM for a in ins]
        for k in far:
            specs[2 + k] = ANY
        return pl.pallas_call(
            body,
            out_shape=outs,
            in_specs=specs,
            out_specs=jax.tree.map(lambda _: out_spec, outs),
            scratch_shapes=scratch,
            compiler_params=pltpu.CompilerParams(vmem_limit_bytes=LIMITS[kind] * MIB),
            cost_estimate=pl.CostEstimate(
                flops=COSTS[kind] * rows * width * products, bytes_accessed=0, transcendentals=0
            ),
        )(logit_scale, logit_bias, *ins)

    hat_type = jax.ShapeDtypeStruct((rows, width), jnp.bfloat16)
    sum_type = jax.ShapeDtypeStruct((rows, width), jnp.float32)
    running = pltpu.VMEM((rows, width), jnp.float32)

    def room(size):
        return pltpu.VMEM((size, width), jnp.bfloat16)

    def named(name, block, pairs):
        with jax.named_scope(name):
            return send(block, pairs)

    def step(kind, take_far, start, hat, base, plain, far_twins, extra=()):
        late = sum(block.shape[0] for block in far_twins)
        size = sum(block.shape[0] for block in plain) + late
        first = 3 + len(plain) + len(far_twins)
        ins = (flag, hat, base, *plain, *far_twins, *(twin if late else ()), *extra)
        body, out, scratch, spec = {
            "half": (half_kernel, sum_type, [room(size)], VMEM),
            "step": (step_kernel, sum_type, [room(size)], VMEM),
            "mid": (mid_kernel, hat_type, [running, room(size)], VMEM),
            "last": (
                last_kernel, (hat_type, hat_type),
                [running, room(size), room(rows), pltpu.SemaphoreType.DMA((1 + n,))], ANY,
            ),
        }[kind]
        if not late:
            return call(kind, body, out, scratch, ins, size, spec)
        body = functools.partial(body, take_far, start, len(plain), len(far_twins))
        if kind != "mid":
            return call(kind, body, out, scratch, ins, size, spec)
        scratch = [*scratch, room(late), pltpu.SemaphoreType.DMA((len(twin),))]
        return call(kind, body, out, scratch, ins, size, spec, range(first, first + len(twin)))

    p1y = [named(f"p1y{k}", v[k], out_y) for k in range(n)]
    p1x = [named(f"p1x{k}", part, over_x) for k, part in enumerate(u)]
    late_text, late_image, *_ = lax.optimization_barrier((text, image, v[0], *u))
    twin = []
    for start in range(0, rows, TWIN):
        here = slice(start, start + TWIN)
        mine = jnp.where(core == 0, late_text[here], late_image[here])
        twin.append(named(f"twin{start}", mine, in_chip))
    u_part = [jnp.where(even, late_text[span], late_image[span]) for span in spans]
    v_own, u_part = lax.optimization_barrier((v, u_part))
    u_hat, v_hat, u_total, v_total = call(
        "own", own_kernel, (hat_type, hat_type, sum_type, sum_type), [], (*u, *v_own), rows * 2
    )
    p1x, v_hat, p1y, twin, u_part = lax.optimization_barrier((p1x, v_hat, p1y, twin, u_part))
    p2x, p2y = [None] * n, [None] * n
    for k in range(n):
        p2x[k] = named(f"p2x{k}", p1y[k], over_x)
        p2y[k] = named(f"p2y{k}", after(u_part[k], p1y[k]), back_y)
    s1x = [named(f"s1x{k}", part, in_chip) for k, part in enumerate(p1x)]
    s1y = [named(f"s1y{k}", p1y[k], in_chip) for k in range(n)]
    u_total = step("half", 1, 0, u_hat, u_total, [*p1x, *p1y], [])
    u_grad = token = step("mid", 1, 0, u_hat, u_total, s1x, s1y, tuple(u))
    for k in range(n):
        near_twin = named(f"s2x{k}", after(p2x[k], token), in_chip)
        far_twin = named(f"s2y{k}", after(p2y[k], token), in_chip)
        plain, start = [p2x[k], p2y[k], near_twin], spans[k].start
        if k < n - 1:
            v_total = token = step("step", 0, start, v_hat, v_total, plain, [far_twin])
        else:
            return step("last", 0, start, v_hat, v_total, plain, [far_twin], (*v, u_grad))


def solution(mesh):
    placed = (P("batch", None), P("batch", None), P(), P())
    return jax.shard_map(
        shards,
        mesh=mesh,
        in_specs=placed,
        out_specs=(P("batch", None), P("batch", None)),
        check_vma=False,
    )
```

```python
import functools

import jax
import jax.numpy as jnp
from jax import lax
from jax.experimental import pallas as pl
from jax.experimental.pallas import tpu as pltpu
from jax.sharding import PartitionSpec as P

EPS = 1e-06
CHUNKS = (512, 256)
ROW_TILE = 256
TWIN = 384
OVER_X = (400, 368)
VMEM = pl.BlockSpec(memory_space=pltpu.VMEM)
SMEM = pl.BlockSpec(memory_space=pltpu.SMEM)
MIB = 1024 * 1024
LIMITS = {"half": 15, "own": 16, "mid": 20, "step": 20, "last": 20}
BLOCK = 1024
COSTS = {"half": 0, "own": 4, "mid": 0, "step": 4, "last": 4}
ANY = pl.BlockSpec(memory_space=pl.ANY)


def unit_rows(raw):
    wide = raw.astype(jnp.float32)
    inv = lax.rsqrt(jnp.sum(wide * wide, axis=-1, keepdims=True) + EPS)
    return wide * inv, inv


def hat_rows(raw):
    return unit_rows(raw)[0].astype(jnp.bfloat16)


def bands(refs):
    at = 0
    for ref in refs:
        count = ref.shape[0]
        for start in range(0, count, ROW_TILE):
            stop = min(start + ROW_TILE, count)
            yield slice(at + start, at + stop), ref, slice(start, stop)
        at += count


def add_tile(total, base, own_hat, other, scale, bias, diagonal=False, block=None):
    rows, count = own_hat.shape[0], other.shape[0]
    if block is not None:
        block = count // 2 if count > 1152 else count
        if block == count:
            add_tile(total, base, own_hat, other, scale, bias)
            return
        total[...] = base[...]

        @pl.loop(0, count // block)
        def _(k):
            part = other.at[pl.ds(pl.multiple_of(k * block, block), block)]
            add_tile(total, total, own_hat, part, scale, bias)

        return
    for start in range(0, rows, ROW_TILE):
        band = slice(start, start + ROW_TILE)
        logits = lax.dot_general(
            own_hat[band, :], other[...], (((1,), (1,)), ((), ())),
            preferred_element_type=jnp.float32,
        )
        coef = jax.nn.sigmoid(scale * logits + bias)
        if diagonal:
            i = lax.broadcasted_iota(jnp.int32, coef.shape, 0) + start
            j = lax.broadcasted_iota(jnp.int32, coef.shape, 1)
            coef = coef - jnp.where(i == j, 1.0, 0.0)
        part = jnp.dot(coef.astype(jnp.bfloat16), other[...], preferred_element_type=jnp.float32)
        total[band, :] = part if base is None else base[band, :] + part


def project_band(grad, total, band, raw, scale):
    unit, inv = unit_rows(raw)
    acc = scale * total[band, :]
    along = jnp.sum(unit * acc, axis=-1, keepdims=True)
    grad[band, :] = (inv * (acc - unit * along)).astype(jnp.bfloat16)


def project_back(grad, total, raw, scale):
    for band, ref, part in bands(raw):
        project_band(grad, total, band, ref[part, :], scale)


def put_hat(hat, raw, at=0):
    rows = raw.shape[0]
    for start in range(0, rows, ROW_TILE):
        stop = min(start + ROW_TILE, rows)
        hat[at + start:at + stop, :] = hat_rows(raw[start:stop, :])


def own_kernel(scale_ref, bias_ref, *refs):
    n, m = len(CHUNKS), len(OVER_X)
    u, v, (u_hat, v_hat, u_total, v_total) = refs[:m], refs[m:m + n], refs[m + n:]
    scale, bias = scale_ref[0], bias_ref[0]
    for hat, parts in ((u_hat, u), (v_hat, v)):
        at = 0
        for part in parts:
            put_hat(hat, part, at)
            at += part.shape[0]
    add_tile(u_total, None, u_hat, v_hat, scale, bias, True)
    add_tile(v_total, None, v_hat, u_hat, scale, bias, True)


def gather_hats(other, flag, take_far, plain, far_twins=(), twin=None, at=0, landing=()):
    row = 0
    for block in plain:
        put_hat(other, block, row)
        row += block.shape[0]
    first = row
    for copy in landing:
        copy.wait()
    for far_twin in far_twins:
        size = far_twin.shape[0]
        start = 0
        while start < size:
            own = row - first + start
            stop = min(size, start + min(ROW_TILE, TWIN - (at + own) % TWIN))
            extra = jnp.where(
                flag[0] == take_far, far_twin[start:stop, :], twin(own, stop - start)
            )
            other[row + start:row + stop, :] = hat_rows(extra)
            start = stop
        row += size


def rows_at(twin, at):
    def read(row, count):
        piece, here = divmod(at + row, TWIN)
        return twin[piece][here:here + count, :]

    return read


def fetch(twin, at, size, spare, sems):
    copies, row = [], 0
    while row < size:
        piece, here = divmod(at + row, TWIN)
        count = min(size - row, TWIN - here)
        copies.append(
            pltpu.make_async_copy(
                twin[piece].at[pl.ds(here, count)], spare.at[pl.ds(row, count)], sems.at[len(copies)]
            )
        )
        row += count
    for copy in copies:
        copy.start()
    return copies


def half_kernel(scale_ref, bias_ref, flag, hat, base, *refs):
    *plain, total, other = refs
    gather_hats(other, flag, 0, plain)
    add_tile(total, base, hat, other, scale_ref[0], bias_ref[0], block=BLOCK)


def step_kernel(take_far, at, count, far, scale_ref, bias_ref, flag, hat, base, *refs):
    plain, far_twins, (*twin, total, other) = refs[:count], refs[count:count + far], refs[count + far:]
    gather_hats(other, flag, take_far, plain, far_twins, rows_at(twin, at), at)
    add_tile(total, base, hat, other, scale_ref[0], bias_ref[0], block=BLOCK)


def mid_kernel(take_far, at, count, far, scale_ref, bias_ref, flag, hat, base, *refs):
    plain, far_twins, refs = refs[:count], refs[count:count + far], refs[count + far:]
    *refs, grad, total, other, spare, pieces = refs
    m = len(OVER_X)
    twin, raw = refs[:-m], refs[-m:]
    landing = fetch(twin, at, spare.shape[0], spare, pieces)
    gather_hats(
        other, flag, take_far, plain, far_twins,
        lambda row, size: spare[row:row + size, :], at, landing,
    )
    add_tile(total, base, hat, other, scale_ref[0], bias_ref[0], block=BLOCK)
    project_back(grad, total, raw, scale_ref[0])


def last_kernel(take_far, at, count, far, scale_ref, bias_ref, flag, hat, base, *refs):
    n = len(CHUNKS)
    plain, far_twins, refs = refs[:count], refs[count:count + far], refs[count + far:]
    *refs, done, image_grad, text_grad, total, other, grad, sems = refs
    twin, raw = refs[:-n], refs[-n:]
    is_image = flag[1] == 0
    scale = scale_ref[0]
    whole = (
        pltpu.make_async_copy(done, text_grad, sems.at[0]),
        pltpu.make_async_copy(done, image_grad, sems.at[0]),
    )

    def each(pair, act):
        @pl.when(is_image)
        def _():
            act(pair[0])

        @pl.when(jnp.logical_not(is_image))
        def _():
            act(pair[1])

    each(whole, lambda copy: copy.start())
    gather_hats(other, flag, take_far, plain, far_twins, rows_at(twin, at), at)
    add_tile(total, base, hat, other, scale, bias_ref[0], block=BLOCK)
    copies, row = [], 0
    for k, ref in enumerate(raw):
        band = slice(row, row + ref.shape[0])
        row += ref.shape[0]
        project_band(grad, total, band, ref[...], scale)
        copies.append((
            pltpu.make_async_copy(grad.at[band], image_grad.at[band], sems.at[1 + k]),
            pltpu.make_async_copy(grad.at[band], text_grad.at[band], sems.at[1 + k]),
        ))
        each(copies[-1], lambda copy: copy.start())
    for pair in (whole, *copies):
        each(pair, lambda copy: copy.wait())


def after(value, *before):
    return lax.optimization_barrier((value, *before))[0]


def shards(image, text, logit_scale, logit_bias):
    devices = lax.axis_size("batch")
    rows, width = image.shape
    me = lax.axis_index("batch")
    core, odd = lax.rem(me, 2), lax.rem(me // 2, 2)
    flag = jnp.stack([jnp.where(core == odd, 0, 1), odd]).astype(jnp.int32)

    def send(block, pairs):
        return lax.ppermute(block, "batch", pairs)

    def is_odd(i):
        return (i // 2) % 2 == 1

    over_x = [(i, i ^ 2) for i in range(devices)]
    out_y = [(i, (i + (4 if is_odd(i) else -4)) % devices) for i in range(devices)]
    back_y = [(i, (i + (-4 if is_odd(i) else 4)) % devices) for i in range(devices)]
    in_chip = [(i, i ^ 1) for i in range(devices)]

    even = odd == 0
    n = len(CHUNKS)
    spans = [slice(sum(CHUNKS[:k]), sum(CHUNKS[:k + 1])) for k in range(n)]
    cuts = [slice(sum(OVER_X[:k]), sum(OVER_X[:k + 1])) for k in range(len(OVER_X))]
    u = [jnp.where(even, text[cut], image[cut]) for cut in cuts]
    v = [jnp.where(even, image[span], text[span]) for span in spans]

    def call(kind, body, outs, scratch, ins, products, out_spec=VMEM, far=()):
        specs = [SMEM, SMEM] + [SMEM if a.ndim == 1 else VMEM for a in ins]
        for k in far:
            specs[2 + k] = ANY
        return pl.pallas_call(
            body,
            out_shape=outs,
            in_specs=specs,
            out_specs=jax.tree.map(lambda _: out_spec, outs),
            scratch_shapes=scratch,
            compiler_params=pltpu.CompilerParams(vmem_limit_bytes=LIMITS[kind] * MIB),
            cost_estimate=pl.CostEstimate(
                flops=COSTS[kind] * rows * width * products, bytes_accessed=0, transcendentals=0
            ),
        )(logit_scale, logit_bias, *ins)

    hat_type = jax.ShapeDtypeStruct((rows, width), jnp.bfloat16)
    sum_type = jax.ShapeDtypeStruct((rows, width), jnp.float32)
    running = pltpu.VMEM((rows, width), jnp.float32)

    def room(size):
        return pltpu.VMEM((size, width), jnp.bfloat16)

    def named(name, block, pairs):
        with jax.named_scope(name):
            return send(block, pairs)

    def step(kind, take_far, start, hat, base, plain, far_twins, extra=()):
        late = sum(block.shape[0] for block in far_twins)
        size = sum(block.shape[0] for block in plain) + late
        first = 3 + len(plain) + len(far_twins)
        ins = (flag, hat, base, *plain, *far_twins, *(twin if late else ()), *extra)
        body, out, scratch, spec = {
            "half": (half_kernel, sum_type, [room(size)], VMEM),
            "step": (step_kernel, sum_type, [room(size)], VMEM),
            "mid": (mid_kernel, hat_type, [running, room(size)], VMEM),
            "last": (
                last_kernel, (hat_type, hat_type),
                [running, room(size), room(rows), pltpu.SemaphoreType.DMA((1 + n,))], ANY,
            ),
        }[kind]
        if not late:
            return call(kind, body, out, scratch, ins, size, spec)
        body = functools.partial(body, take_far, start, len(plain), len(far_twins))
        if kind != "mid":
            return call(kind, body, out, scratch, ins, size, spec)
        scratch = [*scratch, room(late), pltpu.SemaphoreType.DMA((len(twin),))]
        return call(kind, body, out, scratch, ins, size, spec, range(first, first + len(twin)))

    p1y = [named(f"p1y{k}", v[k], out_y) for k in range(n)]
    p1x = [named(f"p1x{k}", part, over_x) for k, part in enumerate(u)]
    late_text, late_image, *_ = lax.optimization_barrier((text, image, v[0], *u))
    twin = []
    for start in range(0, rows, TWIN):
        here = slice(start, start + TWIN)
        mine = jnp.where(core == 0, late_text[here], late_image[here])
        twin.append(named(f"twin{start}", mine, in_chip))
    u_part = [jnp.where(even, late_text[span], late_image[span]) for span in spans]
    v_own, u_part = lax.optimization_barrier((v, u_part))
    u_hat, v_hat, u_total, v_total = call(
        "own", own_kernel, (hat_type, hat_type, sum_type, sum_type), [], (*u, *v_own), rows * 2
    )
    p1x, v_hat, p1y, twin, u_part = lax.optimization_barrier((p1x, v_hat, p1y, twin, u_part))
    p2x, p2y = [None] * n, [None] * n
    for k in range(n):
        p2x[k] = named(f"p2x{k}", p1y[k], over_x)
        p2y[k] = named(f"p2y{k}", after(u_part[k], p1y[k]), back_y)
    s1x = [named(f"s1x{k}", part, in_chip) for k, part in enumerate(p1x)]
    s1y = [named(f"s1y{k}", p1y[k], in_chip) for k in range(n)]
    u_total = step("half", 1, 0, u_hat, u_total, [*p1x, *p1y], [])
    u_grad = token = step("mid", 1, 0, u_hat, u_total, s1x, s1y, tuple(u))
    for k in range(n):
        near_twin = named(f"s2x{k}", after(p2x[k], token), in_chip)
        far_twin = named(f"s2y{k}", after(p2y[k], token), in_chip)
        plain, start = [p2x[k], p2y[k], near_twin], spans[k].start
        if k < n - 1:
            v_total = token = step("step", 0, start, v_hat, v_total, plain, [far_twin])
        else:
            return step("last", 0, start, v_hat, v_total, plain, [far_twin], (*v, u_grad))


def solution(mesh):
    placed = (P("batch", None), P("batch", None), P(), P())
    return jax.shard_map(
        shards,
        mesh=mesh,
        in_specs=placed,
        out_specs=(P("batch", None), P("batch", None)),
        check_vma=False,
    )
```
